32 devices in a mesh: dp: 4 (over x, core), ctx: 8 (over z, y).
Axes of the slice: x: 2, y: 2, z: 4, core: 2. Of those that a mesh axis runs over, the one named last changes fastest.
Arguments:
- queries: bfloat16 [4, 16, 24576], P('dp', 'ctx'), may hold values from -6 to 6
- grad_out: bfloat16 [4, 16, 16384], P('dp', 'ctx'), may hold values from -64 to 64
- latent: bfloat16 [4, 1024, 576], P('dp', 'ctx'), may hold values from -6 to 6
- latent_up: bfloat16 [512, 32768], P(None, 'ctx'), may hold values from -0.25 to 0.25
- query_start: int32 [4], P('dp'), may hold values from 2 to 1008
- key_lengths: int32 [4], P('dp'), may hold values from 18 to 1024, as said below
Outputs:
- grad_queries: float32 [4, 16, 24576], P('dp', 'ctx')
- grad_latent: float32 [4, 1024, 576], P('dp', 'ctx')
- grad_latent_up: float32 [512, 32768], P('dp', 'ctx')
The draws below stay inside these ranges and needn't reach their ends.
Inputs may be any that keep to these rules, and one draw needn't show every extreme that they name: key_lengths[g] is at most query_start[g] + 16.
All inputs are finite; a program needn't handle non-finite values.
Results may differ from the reference program's by a relative error of at most 0.015.
Values may be sent and summed in bfloat16 or wider, within the bound.
A program may use at most 128 MiB of HBM per device.

```python
import math
import jax
import jax.numpy as jnp
from jax import lax

H = 128
DN = 128
DR = 64
DV = 128
C = 512
Q = 16
L = 1024
GROUPS = 4
N_CTX = 8


def windows(key):
    base_key = jax.random.fold_in(key, 101)
    first_key, second_key, third_key = jax.random.split(base_key, 3)
    starts = jax.random.randint(first_key, (GROUPS,), 2, L - Q + 1)
    lengths = jax.random.randint(second_key, (GROUPS,), Q + 2, starts + Q + 1)
    widest = jax.random.randint(third_key, (), 0, GROUPS)
    picked = jnp.arange(GROUPS) == widest
    starts = jnp.where(picked, L - Q, starts)
    lengths = jnp.where(picked, L, lengths)
    return (starts.astype(jnp.int32), lengths.astype(jnp.int32))


def draw_query_start(key, part):
    return windows(key)[0]


def draw_key_lengths(key, part):
    return windows(key)[1]


def draw_queries(key, part):
    own_key = jax.random.fold_in(key, 202)
    full_shape = (GROUPS, Q, H, DN + DR)
    values = jnp.clip(jax.random.normal(own_key, full_shape, jnp.float32), -6.0, 6.0)
    return values.reshape(GROUPS, Q, H * (DN + DR)).astype(jnp.bfloat16)


def draw_latent(key, part):
    own_key = jax.random.fold_in(key, 303)
    full_shape = (GROUPS, L, C + DR)
    values = jnp.clip(jax.random.normal(own_key, full_shape, jnp.float32), -6.0, 6.0)
    return values.astype(jnp.bfloat16)


def block_scale(key, extent, pieces, smallest, high):
    factor_of, own = 1.0, jax.random.fold_in(key, 6)
    for axis_at, shards_of in pieces:
        heights = jnp.exp(jax.random.uniform(jax.random.fold_in(own, axis_at), (shards_of,), jnp.float32, smallest / len(pieces), high / len(pieces)))
        factor_of = factor_of * jnp.repeat(heights, extent[axis_at] // shards_of).reshape([-1 if axis == axis_at else 1 for axis in range(len(extent))])
    return factor_of


def scatter_about(key, dims, width, reach, pieces=(), kind=jnp.bfloat16):
    gain = block_scale(key, dims, pieces, -0.22, 0.18) if pieces else 1.0
    array = jax.random.normal(key, dims, jnp.float32) * width * gain
    return jnp.minimum(jnp.maximum(array, -reach), reach).astype(kind)


def setup_inputs(seed: int = 0) -> dict:
    streams_of = jax.random.split(jax.random.key(seed), 7)
    queries = draw_queries(jax.random.fold_in(streams_of[6], 71), 0)
    grad_out = jnp.clip(jax.random.uniform(streams_of[1], (GROUPS, Q, H * DV), jnp.float32, -64.0, 64.0) * block_scale(streams_of[1], (GROUPS, Q, H * DV), ((0, 4), (1, 8)), -0.4, 0.0), -64.0, 64.0).astype(jnp.bfloat16)
    latent = draw_latent(jax.random.fold_in(streams_of[6], 71), 0)
    latent_up = scatter_about(streams_of[3], (C, H * (DN + DV)), C ** -0.5, 0.25, ((1, 8),))
    query_start = draw_query_start(jax.random.fold_in(streams_of[6], 71), 0)
    key_lengths = draw_key_lengths(jax.random.fold_in(streams_of[6], 71), 0)
    return {"queries": queries, "grad_out": grad_out, "latent": latent, "latent_up": latent_up, "query_start": query_start, "key_lengths": key_lengths}


MSCALE = 0.1 * math.log(40.0) + 1.0
NEG_FILL = -1e+30

def lowered(values):
    return lax.optimization_barrier(values.astype(jnp.bfloat16)).astype(jnp.float32)

def head_group(q_part, g_part, w_part, all_keys, visible, score_scale):
    q_nope = q_part[:, :, :DN]
    q_rope = q_part[:, :, DN:]
    w_key = w_part[:, :, :DN].astype(jnp.float32)
    w_value = w_part[:, :, DN:].astype(jnp.float32)
    q_latent = lowered(jnp.einsum('qhd,chd->qhc', q_nope.astype(jnp.float32), w_key))
    g_latent = lowered(jnp.einsum('qhd,chd->qhc', g_part.astype(jnp.float32), w_value))
    q_full = jnp.concatenate([q_latent, q_rope.astype(jnp.float32)], axis=2)
    key_float = all_keys.astype(jnp.float32)
    raw = score_scale * jnp.einsum('qhc,kc->qhk', q_full, key_float)
    seen = visible[:, None, :]
    masked = jnp.where(seen, raw, NEG_FILL)
    row_peak = lax.optimization_barrier(jnp.max(masked, axis=2, keepdims=True))
    weights = jnp.where(seen, jnp.exp(masked - row_peak), 0.0)
    attn = weights / lax.optimization_barrier(jnp.sum(weights, axis=2, keepdims=True))
    attn_low = lowered(attn)
    o_latent = jnp.einsum('qhk,kc->qhc', attn_low, key_float[:, :C])
    grad_probs = jnp.einsum('qhc,kc->qhk', g_latent, key_float[:, :C])
    row_dot = lax.optimization_barrier(jnp.sum(attn_low * grad_probs, axis=2, keepdims=True))
    grad_scores = lowered(score_scale * attn * (grad_probs - row_dot))
    query_grad = jnp.einsum('qhk,kc->qhc', grad_scores, key_float)
    key_side = jnp.einsum('qhk,qhc->kc', grad_scores, q_full)
    value_side = jnp.einsum('qhk,qhc->kc', attn_low, g_latent)
    key_term = lowered(key_side + jnp.pad(value_side, ((0, 0), (0, DR))))
    grad_lat = lowered(query_grad[:, :, :C])
    grad_nope = jnp.einsum('qhc,chd->qhd', grad_lat, w_key)
    grad_query = jnp.concatenate([grad_nope, query_grad[:, :, C:]], axis=2)
    key_weight = jnp.einsum('qhc,qhd->chd', grad_lat, q_nope.astype(jnp.float32))
    value_weight = jnp.einsum('qhc,qhd->chd', lowered(o_latent), g_part.astype(jnp.float32))
    return (grad_query, key_term, jnp.concatenate([key_weight, value_weight], axis=2))

def reference(queries, grad_out, latent, latent_up, query_start, key_lengths):
    score_scale = MSCALE * MSCALE / math.sqrt(DN + DR)
    heads_dev = H // N_CTX
    weight_parts = latent_up.reshape(C, N_CTX, heads_dev, DN + DV).transpose(1, 0, 2, 3)
    key_pos = jnp.arange(L, dtype=jnp.int32)
    query_off = jnp.arange(Q, dtype=jnp.int32)

    def one_group(weight_total, inputs):
        q_group, g_group, key_group, slice_start, key_len = inputs
        window_low = slice_start + Q - key_len
        visible = (key_pos[None, :] >= window_low) & (key_pos[None, :] <= slice_start + query_off[:, None])
        q_parts = q_group.reshape(Q, N_CTX, heads_dev, DN + DR).transpose(1, 0, 2, 3)
        g_parts = g_group.reshape(Q, N_CTX, heads_dev, DV).transpose(1, 0, 2, 3)

        def one_part(key_total, part):
            q_part, g_part, w_part = part
            grad_query, key_term, weight_term = head_group(q_part, g_part, w_part, key_group, visible, score_scale)
            return (key_total + key_term, (grad_query, weight_term))
        key_total, (query_grads, weight_terms) = lax.scan(one_part, jnp.zeros((L, C + DR), jnp.float32), (q_parts, g_parts, weight_parts))
        grad_rows = query_grads.transpose(1, 0, 2, 3).reshape(Q, H * (DN + DR))
        weight_sum = weight_terms.transpose(1, 0, 2, 3).reshape(C, H * (DN + DV))
        return (weight_total + weight_sum, (grad_rows, key_total))
    weight_total, (grad_queries, grad_latent) = lax.scan(one_group, jnp.zeros((C, H * (DN + DV)), jnp.float32), (queries, grad_out, latent, query_start, key_lengths))
    return (grad_queries, grad_latent, weight_total)
```

```python
import functools
import math

import jax
import jax.numpy as jnp
from jax import lax
from jax.experimental import pallas as pl
from jax.experimental.pallas import tpu as pltpu
from jax.sharding import PartitionSpec as P

DN = 128
DR = 64
DV = 128
C = 512

MSCALE = 0.1 * math.log(40.0) + 1.0
NEG_FILL = -1e30
SCALE = MSCALE * MSCALE / math.sqrt(DN + DR)
CHUNKS = 2
MESH = pl.DeviceIdType.MESH
F32 = jnp.float32
BF16 = jnp.bfloat16


def dot(a, b, da, db):
    return lax.dot_general(a, b, (((da,), (db,)), ((), ())), preferred_element_type=F32)


def grid_of(n):
    inner = 1
    while (2 * inner) ** 2 <= n and n % (2 * inner) == 0:
        inner *= 2
    return n // inner, inner


def kernel(
    n_dp, n_ctx, start_ref, length_ref, q_ref, g_ref, lat_ref, w_hbm,
    gq_out, gl_out, gw_out,
    w, q_recv, g_recv, q_rows, g_rows, nope, gout, q_full, g_lat, keys,
    probs_all, grads_all, o_low, grad_lat, rope_grad,
    wg, core_recv, x_send, x_recv,
    kt_send, kt_recv, kt_own, z_send, z_recv,
    gq_rows, gq_send, gq_recv,
    w_sem, q_ss, q_rs, g_ss, g_rs, az_ss, az_rs, ay_ss, ay_rs,
    c_ss, c_rs, x_ss, x_rs, ky_ss, ky_rs, kz_ss, kz_rs, o_ss, o_rs,
):
    nz, ny = grid_of(n_ctx)
    ncore = 2 if n_dp % 2 == 0 else 1
    nx = n_dp // ncore
    dp = lax.axis_index("dp")
    me = lax.axis_index("ctx")
    z, y = me // ny, me % ny
    x, core = dp // ncore, dp % ncore
    other = (core + 1) % ncore
    rq = q_ref.shape[1]
    nq = rq * n_ctx
    wq = q_ref.shape[2] // n_ctx
    wv = g_ref.shape[2] // n_ctx
    heads = wv // DV
    rows = heads * nq
    lb = lat_ref.shape[1]
    nk = lb * n_ctx
    cr = C // n_dp

    def ctx_dev(i):
        return (dp, i)

    def dp_dev(xi, ci):
        return (xi * ncore + ci, me)

    def copy(src, dst, ss, rs, dev):
        return pltpu.make_async_remote_copy(
            src_ref=src, dst_ref=dst, send_sem=ss, recv_sem=rs, device_id=dev, device_id_type=MESH
        )

    w_copy = pltpu.make_async_copy(w_hbm, w, w_sem)
    w_copy.start()

    barrier = pltpu.get_barrier_semaphore()
    peers = [ctx_dev((me + d) % n_ctx) for d in range(1, n_ctx)]
    peers += [dp_dev((x + d) % nx, core) for d in range(1, nx)]
    if ncore > 1:
        peers.append(dp_dev(x, other))
    for dev in peers:
        pl.semaphore_signal(barrier, inc=1, device_id=dev, device_id_type=MESH)
    pl.semaphore_wait(barrier, len(peers))

    sends = []
    for d in range(1, n_ctx):
        j = (me + d) % n_ctx
        at = pl.ds(pl.multiple_of(j * wq, 128), wq)
        sends.append(copy(q_ref.at[0, :, at], q_recv.at[me], q_ss.at[d - 1], q_rs.at[d - 1], ctx_dev(j)))
        at = pl.ds(pl.multiple_of(j * wv, 128), wv)
        sends.append(copy(g_ref.at[0, :, at], g_recv.at[me], g_ss.at[d - 1], g_rs.at[d - 1], ctx_dev(j)))
    for s in sends:
        s.start()
    for d in range(1, nz):
        to = ((z + d) % nz) * ny + y
        s = copy(lat_ref.at[0], keys.at[me], az_ss.at[d - 1], az_rs.at[d - 1], ctx_dev(to))
        s.start()
        sends.append(s)

    def forward(k, src, block):
        for d in range(1, ny):
            to = z * ny + (y + d) % ny
            i = (d - 1) * nz + k
            s = copy(src, keys.at[block], ay_ss.at[i], ay_rs.at[i], ctx_dev(to))
            s.start()
            sends.append(s)

    forward(0, lat_ref.at[0], me)
    keys[me] = lat_ref[0]
    q_recv[me] = q_ref[0, :, pl.ds(pl.multiple_of(me * wq, 128), wq)]
    g_recv[me] = g_ref[0, :, pl.ds(pl.multiple_of(me * wv, 128), wv)]

    for d in range(1, n_ctx):
        j = (me - d + n_ctx) % n_ctx
        copy(q_recv.at[j], q_recv.at[j], q_ss.at[d - 1], q_rs.at[d - 1], ctx_dev(j)).wait_recv()
        copy(g_recv.at[j], g_recv.at[j], g_ss.at[d - 1], g_rs.at[d - 1], ctx_dev(j)).wait_recv()
    for j in range(n_ctx):
        q_rows[rq * j : rq * (j + 1), :] = q_recv[j].astype(F32)
        g_rows[rq * j : rq * (j + 1), :] = g_recv[j].astype(F32)
    w_copy.wait()

    def latents(h):
        at = slice(h * nq, (h + 1) * nq)
        qh = q_rows[:, h * (DN + DR) : (h + 1) * (DN + DR)].astype(BF16)
        gh = g_rows[:, h * DV : (h + 1) * DV].astype(BF16)
        nope[h] = qh[:, :DN]
        gout[h] = gh
        col = h * (DN + DV)
        q_full[at, :C] = dot(qh[:, :DN], w[:, col : col + DN], 1, 1).astype(BF16)
        q_full[at, C:] = qh[:, DN:]
        g_lat[at, :] = dot(gh, w[:, col + DN : col + DN + DV], 1, 1).astype(BF16)

    per = -(-heads // nz)
    for h in range(heads):
        latents(h)
        d = (h + 1) // per
        if (h + 1) % per == 0 and d < nz:
            block = ((z - d + nz) % nz) * ny + y
            copy(keys.at[block], keys.at[block], az_ss.at[d - 1], az_rs.at[d - 1], ctx_dev(block)).wait_recv()
            forward(d, keys.at[block], block)
    for d in range(heads // per + 1 if heads // per < nz else nz, nz):
        block = ((z - d + nz) % nz) * ny + y
        copy(keys.at[block], keys.at[block], az_ss.at[d - 1], az_rs.at[d - 1], ctx_dev(block)).wait_recv()
        forward(d, keys.at[block], block)
    for k in range(nz):
        for d in range(1, ny):
            block = ((z - k + nz) % nz) * ny + (y - d + ny) % ny
            i = (d - 1) * nz + k
            copy(keys.at[block], keys.at[block], ay_ss.at[i], ay_rs.at[i], ctx_dev(block)).wait_recv()

    start = start_ref[0]
    low = start + nq - length_ref[0]
    hc = heads // CHUNKS
    rc = hc * nq
    cw = hc * (DN + DV)

    def attend(c):
        at = slice(c * rc, (c + 1) * rc)
        all_keys = keys[...].reshape(nk, C + DR)
        raw = dot(q_full[at, :], all_keys, 1, 1) * SCALE
        key_pos = lax.broadcasted_iota(jnp.int32, (rc, nk), 1)
        row_pos = start + lax.broadcasted_iota(jnp.int32, (rc, nk), 0) % nq
        visible = (key_pos >= low) & (key_pos <= row_pos)
        masked = jnp.where(visible, raw, NEG_FILL)
        peak = jnp.max(masked, axis=1, keepdims=True)
        weights = jnp.where(visible, jnp.exp(masked - peak), 0.0)
        attn = weights * (1.0 / jnp.sum(weights, axis=1, keepdims=True))
        probs_low = attn.astype(BF16)
        probs_all[at, :] = probs_low
        o_low[at, :] = dot(probs_low, all_keys[:, :C], 1, 0).astype(BF16)
        grad_probs = dot(g_lat[at, :], all_keys[:, :C], 1, 1)
        row_dot = jnp.sum(probs_low.astype(F32) * grad_probs, axis=1, keepdims=True)
        grads = (SCALE * attn * (grad_probs - row_dot)).astype(BF16)
        grads_all[at, :] = grads
        query_grad = dot(grads, all_keys, 1, 0)
        grad_lat[at, :] = query_grad[:, :C].astype(BF16)
        rope_grad[at, :] = query_grad[:, C:]

    def weight_grads(c):
        for i in range(hc):
            h = c * hc + i
            at = slice(h * nq, (h + 1) * nq)
            col = i * (DN + DV)
            key_w = dot(grad_lat[at, :], nope[h], 0, 0).astype(BF16)
            value_w = dot(o_low[at, :], gout[h], 0, 0).astype(BF16)
            for b in range(n_dp):
                part = slice(b * cr, (b + 1) * cr)
                wg[c, b % ncore, b // ncore, :, col : col + DN] = key_w[part]
                wg[c, b % ncore, b // ncore, :, col + DN : col + DN + DV] = value_w[part]
        if ncore > 1:
            s = copy(wg.at[c, other], core_recv.at[c], c_ss.at[c], c_rs.at[c], dp_dev(x, other))
            s.start()
            sends.append(s)

    def core_sum(c, xi):
        own = wg[c, core, xi].astype(F32)
        if ncore > 1:
            own = own + core_recv[c, xi].astype(F32)
        return own

    def across_x(c):
        if ncore > 1:
            copy(core_recv.at[c], core_recv.at[c], c_ss.at[c], c_rs.at[c], dp_dev(x, other)).wait_recv()
        for d in range(1, nx):
            xi = (x + d) % nx
            i = c * (nx - 1) + d - 1
            x_send[i] = core_sum(c, xi).astype(BF16)
            s = copy(x_send.at[i], x_recv.at[i], x_ss.at[i], x_rs.at[i], dp_dev(xi, core))
            s.start()
            sends.append(s)

    def key_block(block):
        cols = pl.ds(pl.multiple_of(block * lb, lb), lb)
        key_side = dot(grads_all[:, cols], q_full[...], 0, 0)
        value_side = dot(probs_all[:, cols], g_lat[...], 0, 0)
        return key_side[:, :C] + value_side, key_side[:, C:]

    for c in range(CHUNKS):
        attend(c)
        if c:
            across_x(c - 1)
        weight_grads(c)

    for k in range(nz):
        for d in range(1, ny):
            yi = (y + d) % ny
            block = ((z + k + 1) % nz) * ny + yi
            i = (d - 1) * nz + k
            left, right = key_block(block)
            kt_send[i, :, :C] = left.astype(BF16)
            kt_send[i, :, C:] = right.astype(BF16)
            s = copy(kt_send.at[i], kt_recv.at[i], ky_ss.at[i], ky_rs.at[i], ctx_dev(z * ny + yi))
            s.start()
            sends.append(s)
    across_x(CHUNKS - 1)
    for k in range(nz):
        left, right = key_block(((z + k + 1) % nz) * ny + y)
        kt_own[k, :, :C] = left
        kt_own[k, :, C:] = right

    def inner_sum(k):
        total = kt_own[k]
        for d in range(1, ny):
            i = (d - 1) * nz + k
            copy(kt_recv.at[i], kt_recv.at[i], ky_ss.at[i], ky_rs.at[i], ctx_dev(me)).wait_recv()
            total = total + kt_recv[i].astype(F32)
        return total

    for k in range(nz - 1):
        z_send[k] = inner_sum(k).astype(BF16)
        to = ((z + k + 1) % nz) * ny + y
        s = copy(z_send.at[k], z_recv.at[k], kz_ss.at[k], kz_rs.at[k], ctx_dev(to))
        s.start()
        sends.append(s)

    for h in range(heads):
        at = slice(h * nq, (h + 1) * nq)
        col = h * (DN + DV)
        to = h * (DN + DR)
        gq_rows[:, to : to + DN] = dot(grad_lat[at, :], w[:, col : col + DN], 1, 0)
        gq_rows[:, to + DN : to + DN + DR] = rope_grad[at, :]
    for j in range(n_ctx):
        gq_send[j] = gq_rows[rq * j : rq * (j + 1), :]
    for d in range(1, n_ctx):
        j = (me + d) % n_ctx
        s = copy(gq_send.at[j], gq_recv.at[me], o_ss.at[d - 1], o_rs.at[d - 1], ctx_dev(j))
        s.start()
        sends.append(s)
    gq_recv[me] = gq_send[me]

    total = inner_sum(nz - 1)
    for k in range(nz - 1):
        copy(z_recv.at[k], z_recv.at[k], kz_ss.at[k], kz_rs.at[k], ctx_dev(me)).wait_recv()
        total = total + z_recv[k].astype(F32)
    gl_out[0] = total

    for d in range(1, n_ctx):
        j = (me - d + n_ctx) % n_ctx
        copy(gq_recv.at[j], gq_recv.at[j], o_ss.at[d - 1], o_rs.at[d - 1], ctx_dev(j)).wait_recv()
    for j in range(n_ctx):
        gq_out[0, :, j * wq : (j + 1) * wq] = gq_recv[j]

    for c in range(CHUNKS):
        part = core_sum(c, x)
        for d in range(1, nx):
            i = c * (nx - 1) + d - 1
            copy(x_recv.at[i], x_recv.at[i], x_ss.at[i], x_rs.at[i], dp_dev(x, core)).wait_recv()
            part = part + x_recv[i].astype(F32)
        gw_out[:, c * cw : (c + 1) * cw] = part
    for s in sends:
        s.wait_send()


def local(n_dp, n_ctx, queries, grad_out, latent, latent_up, query_start, key_lengths):
    nz, ny = grid_of(n_ctx)
    ncore = 2 if n_dp % 2 == 0 else 1
    nx = n_dp // ncore
    rq = queries.shape[1]
    nq = rq * n_ctx
    wq = queries.shape[2] // n_ctx
    wv = grad_out.shape[2] // n_ctx
    heads = wv // DV
    rows = heads * nq
    lb = latent.shape[1]
    nk = lb * n_ctx
    cr = C // n_dp
    cw = latent_up.shape[1] // CHUNKS
    full = C + DR
    vm = pltpu.VMEM
    dma = pltpu.SemaphoreType.DMA
    spec = pl.BlockSpec(memory_space=pltpu.VMEM)
    smem = pl.BlockSpec(memory_space=pltpu.SMEM)
    n1 = n_ctx - 1
    ys = max((ny - 1) * nz, 1)
    zs = max(nz - 1, 1)
    xs = max((nx - 1) * CHUNKS, 1)
    return pl.pallas_call(
        functools.partial(kernel, n_dp, n_ctx),
        out_shape=(
            jax.ShapeDtypeStruct(queries.shape, F32),
            jax.ShapeDtypeStruct(latent.shape, F32),
            jax.ShapeDtypeStruct((cr, latent_up.shape[1]), F32),
        ),
        in_specs=[smem, smem, spec, spec, spec, pl.BlockSpec(memory_space=pl.ANY)],
        out_specs=(spec, spec, spec),
        scratch_shapes=[
            vm(latent_up.shape, BF16),
            vm((n_ctx, rq, wq), BF16),
            vm((n_ctx, rq, wv), BF16),
            vm((nq, wq), F32),
            vm((nq, wv), F32),
            vm((heads, nq, DN), BF16),
            vm((heads, nq, DV), BF16),
            vm((rows, full), BF16),
            vm((rows, C), BF16),
            vm((n_ctx, lb, full), BF16),
            vm((rows, nk), BF16),
            vm((rows, nk), BF16),
            vm((rows, C), BF16),
            vm((rows, C), BF16),
            vm((rows, DR), F32),
            vm((CHUNKS, ncore, nx, cr, cw), BF16),
            vm((CHUNKS, nx, cr, cw), BF16),
            vm((xs, cr, cw), BF16),
            vm((xs, cr, cw), BF16),
            vm((ys, lb, full), BF16),
            vm((ys, lb, full), BF16),
            vm((nz, lb, full), F32),
            vm((zs, lb, full), BF16),
            vm((zs, lb, full), BF16),
            vm((nq, wq), F32),
            vm((n_ctx, rq, wq), F32),
            vm((n_ctx, rq, wq), F32),
            dma,
            dma((n1,)), dma((n1,)), dma((n1,)), dma((n1,)),
            dma((zs,)), dma((zs,)), dma((ys,)), dma((ys,)),
            dma((CHUNKS,)), dma((CHUNKS,)), dma((xs,)), dma((xs,)),
            dma((ys,)), dma((ys,)), dma((zs,)), dma((zs,)),
            dma((n1,)), dma((n1,)),
        ],
        compiler_params=pltpu.CompilerParams(
            collective_id=0, has_side_effects=True, vmem_limit_bytes=60 * 1024 * 1024
        ),
    )(query_start, key_lengths, queries, grad_out, latent, latent_up)


def solution(mesh):
    return jax.shard_map(
        functools.partial(local, mesh.shape["dp"], mesh.shape["ctx"]),
        mesh=mesh,
        in_specs=(
            P("dp", "ctx", None),
            P("dp", "ctx", None),
            P("dp", "ctx", None),
            P(None, "ctx"),
            P("dp"),
            P("dp"),
        ),
        out_specs=(P("dp", "ctx", None), P("dp", "ctx", None), P("dp", "ctx")),
        check_vma=False,
    )
```

```python
import functools
import math

import jax
import jax.numpy as jnp
from jax import lax
from jax.experimental import pallas as pl
from jax.experimental.pallas import tpu as pltpu
from jax.sharding import PartitionSpec as P

DN = 128
DR = 64
DV = 128
C = 512

MSCALE = 0.1 * math.log(40.0) + 1.0
NEG_FILL = -1e30
SCALE = MSCALE * MSCALE / math.sqrt(DN + DR)
MESH = pl.DeviceIdType.MESH
F32 = jnp.float32
BF16 = jnp.bfloat16


def dot(a, b, da, db):
    return lax.dot_general(a, b, (((da,), (db,)), ((), ())), preferred_element_type=F32)


def grid_of(n):
    inner = 1
    while (2 * inner) ** 2 <= n and n % (2 * inner) == 0:
        inner *= 2
    return n // inner, inner


def kernel(
    n_dp, n_ctx, start_ref, length_ref, q_ref, g_ref, lat_ref, w_hbm,
    gq_out, gl_out, fac_out, qg_out,
    w, q_recv, g_recv, q_rows, g_rows, qg_all, q_full, g_lat, sides_t, keys,
    raw, grad_probs, low_all, grad_lat, rope_grad, fac_send, fac_all,
    kt_send, kt_recv, kt_own, z_send, z_recv, gq_rows, gq_send, gq_recv,
    w_sem, q_ss, q_rs, g_ss, g_rs, az_ss, az_rs, ay_ss, ay_rs,
    e_ss, e_rs, f_ss, f_rs, ky_ss, ky_rs, kz_ss, kz_rs, o_ss, o_rs,
):
    nz, ny = grid_of(n_ctx)
    dp = lax.axis_index("dp")
    me = lax.axis_index("ctx")
    z, y = me // ny, me % ny
    rq = q_ref.shape[1]
    nq = rq * n_ctx
    wq = q_ref.shape[2] // n_ctx
    wv = g_ref.shape[2] // n_ctx
    heads = wv // DV
    rows = heads * nq
    lb = lat_ref.shape[2]
    nk = lb * n_ctx
    cr = C // n_dp

    def ctx_dev(i):
        return (dp, i)

    def dp_dev(i):
        return (i, me)

    def copy(src, dst, ss, rs, dev):
        return pltpu.make_async_remote_copy(
            src_ref=src, dst_ref=dst, send_sem=ss, recv_sem=rs, device_id=dev, device_id_type=MESH
        )

    def cols(block):
        return pl.ds(pl.multiple_of(block * lb, lb), lb)

    w_copy = pltpu.make_async_copy(w_hbm, w, w_sem)
    w_copy.start()

    barrier = pltpu.get_barrier_semaphore()
    peers = [ctx_dev((me + d) % n_ctx) for d in range(1, n_ctx)]
    peers += [dp_dev((dp + d) % n_dp) for d in range(1, n_dp)]
    for dev in peers:
        pl.semaphore_signal(barrier, inc=1, device_id=dev, device_id_type=MESH)
    pl.semaphore_wait(barrier, len(peers))

    sends = []

    def send(*args):
        s = copy(*args)
        s.start()
        sends.append(s)

    for d in range(1, n_ctx):
        j = (me + d) % n_ctx
        at = pl.ds(pl.multiple_of(j * wq, 128), wq)
        send(q_ref.at[0, :, at], q_recv.at[me], q_ss.at[d - 1], q_rs.at[d - 1], ctx_dev(j))
        at = pl.ds(pl.multiple_of(j * wv, 128), wv)
        send(g_ref.at[0, :, at], g_recv.at[me], g_ss.at[d - 1], g_rs.at[d - 1], ctx_dev(j))

    def forward(k, src, block):
        for d in range(1, ny):
            to = z * ny + (y + d) % ny
            i = (d - 1) * nz + k
            send(src, keys.at[:, cols(block)], ay_ss.at[i], ay_rs.at[i], ctx_dev(to))

    for d in range(1, nz):
        to = ((z + d) % nz) * ny + y
        send(lat_ref.at[0], keys.at[:, cols(me)], az_ss.at[d - 1], az_rs.at[d - 1], ctx_dev(to))
    forward(0, lat_ref.at[0], me)

    def outer_in(d):
        block = ((z - d + nz) % nz) * ny + y
        ref = keys.at[:, cols(block)]
        copy(ref, ref, az_ss.at[d - 1], az_rs.at[d - 1], ctx_dev(block)).wait_recv()
        forward(d, ref, block)

    keys[:, cols(me)] = lat_ref[0]
    q_recv[me] = q_ref[0, :, pl.ds(pl.multiple_of(me * wq, 128), wq)]
    g_recv[me] = g_ref[0, :, pl.ds(pl.multiple_of(me * wv, 128), wv)]
    for d in range(1, n_ctx):
        j = (me - d + n_ctx) % n_ctx
        copy(q_recv.at[j], q_recv.at[j], q_ss.at[d - 1], q_rs.at[d - 1], ctx_dev(j)).wait_recv()
        copy(g_recv.at[j], g_recv.at[j], g_ss.at[d - 1], g_rs.at[d - 1], ctx_dev(j)).wait_recv()
    for j in range(n_ctx):
        q_rows[rq * j : rq * (j + 1), :] = q_recv[j].astype(F32)
        g_rows[rq * j : rq * (j + 1), :] = g_recv[j].astype(F32)
    w_copy.wait()

    def latents(h):
        at = slice(h * nq, (h + 1) * nq)
        qh = q_rows[:, h * (DN + DR) : (h + 1) * (DN + DR)].astype(BF16)
        gh = g_rows[:, h * DV : (h + 1) * DV].astype(BF16)
        qg_all[dp, h, :, :DN] = qh[:, :DN]
        qg_all[dp, h, :, DN:] = gh
        col = h * (DN + DV)
        q_full[at, :C] = dot(qh[:, :DN], w[:, col : col + DN], 1, 1).astype(BF16)
        q_full[at, C:] = qh[:, DN:]
        g_lat[at, :] = dot(gh, w[:, col + DN : col + DN + DV], 1, 1).astype(BF16)

    done = 1
    per = -(-heads // nz)
    for h in range(heads):
        latents(h)
        if (h + 1) % per == 0 and done < nz:
            outer_in(done)
            done += 1
    for d in range(1, n_dp):
        send(qg_all.at[dp], qg_all.at[dp], e_ss.at[d - 1], e_rs.at[d - 1], dp_dev((dp + d) % n_dp))
    for d in range(done, nz):
        outer_in(d)

    def score_block(block):
        at = cols(block)
        part = keys[:, at]
        raw[:, at] = dot(q_full[...], part, 1, 0)
        grad_probs[:, at] = dot(g_lat[...], part[:C], 1, 0)

    for k in range(nz):
        score_block(((z - k + nz) % nz) * ny + y)
    sides_t[:C, :rows] = q_full[:, :C].T
    sides_t[C:, :rows] = q_full[:, C:].T
    sides_t[:C, rows:] = g_lat[...].T
    sides_t[C:, rows:] = jnp.zeros((DR, rows), BF16)
    for k in range(nz):
        for d in range(1, ny):
            block = ((z - k + nz) % nz) * ny + (y - d + ny) % ny
            i = (d - 1) * nz + k
            ref = keys.at[:, cols(block)]
            copy(ref, ref, ay_ss.at[i], ay_rs.at[i], ctx_dev(block)).wait_recv()
            score_block(block)

    start = start_ref[0]
    low = start + nq - length_ref[0]
    rc = max(nq, 32)
    for c in range(rows // rc):
        at = slice(c * rc, (c + 1) * rc)
        key_pos = lax.broadcasted_iota(jnp.int32, (rc, nk), 1)
        row_pos = start + lax.broadcasted_iota(jnp.int32, (rc, nk), 0) % nq
        visible = (key_pos >= low) & (key_pos <= row_pos)
        masked = jnp.where(visible, raw[at, :] * SCALE, NEG_FILL)
        peak = jnp.max(masked, axis=1, keepdims=True)
        weights = jnp.where(visible, jnp.exp(masked - peak), 0.0)
        attn = weights * (1.0 / jnp.sum(weights, axis=1, keepdims=True))
        probs_low = attn.astype(BF16)
        gp = grad_probs[at, :]
        row_dot = jnp.sum(probs_low.astype(F32) * gp, axis=1, keepdims=True)
        low_all[at, :] = (SCALE * attn * (gp - row_dot)).astype(BF16)
        low_all[rows + c * rc : rows + (c + 1) * rc, :] = probs_low

    def key_block(block):
        return dot(sides_t[...], low_all[:, cols(block)], 1, 0)

    for k in range(nz):
        for d in range(1, ny):
            yi = (y + d) % ny
            i = (d - 1) * nz + k
            kt_send[i] = key_block(((z + k + 1) % nz) * ny + yi).astype(BF16)
            send(kt_send.at[i], kt_recv.at[i], ky_ss.at[i], ky_rs.at[i], ctx_dev(z * ny + yi))

    query_grad = dot(low_all[:rows, :], keys[...], 1, 1)
    rope_grad[...] = query_grad[:, C:]
    grad_lat[...] = query_grad[:, :C].astype(BF16)
    o_low = dot(low_all[rows:, :], keys[:C, :], 1, 1).astype(BF16)
    for b in range(n_dp):
        fac_send[b, :, :cr] = grad_lat[:, b * cr : (b + 1) * cr]
        fac_send[b, :, cr:] = o_low[:, b * cr : (b + 1) * cr]
    for d in range(1, n_dp):
        b = (dp + d) % n_dp
        send(fac_send.at[b], fac_all.at[dp], f_ss.at[d - 1], f_rs.at[d - 1], dp_dev(b))
    fac_all[dp] = fac_send[dp]

    def inner_sum(k):
        total = kt_own[k]
        for d in range(1, ny):
            i = (d - 1) * nz + k
            copy(kt_recv.at[i], kt_recv.at[i], ky_ss.at[i], ky_rs.at[i], ctx_dev(me)).wait_recv()
            total = total + kt_recv[i].astype(F32)
        return total

    for k in range(nz):
        kt_own[k] = key_block(((z + k + 1) % nz) * ny + y)
    for k in range(nz - 1):
        z_send[k] = inner_sum(k).astype(BF16)
        to = ((z + k + 1) % nz) * ny + y
        send(z_send.at[k], z_recv.at[k], kz_ss.at[k], kz_rs.at[k], ctx_dev(to))

    for h in range(heads):
        at = slice(h * nq, (h + 1) * nq)
        col = h * (DN + DV)
        to = h * (DN + DR)
        gq_rows[:, to : to + DN] = dot(grad_lat[at, :], w[:, col : col + DN], 1, 0)
        gq_rows[:, to + DN : to + DN + DR] = rope_grad[at, :]
    for j in range(n_ctx):
        gq_send[j] = gq_rows[rq * j : rq * (j + 1), :]
    for d in range(1, n_ctx):
        j = (me + d) % n_ctx
        send(gq_send.at[j], gq_recv.at[me], o_ss.at[d - 1], o_rs.at[d - 1], ctx_dev(j))
    gq_recv[me] = gq_send[me]

    for d in range(1, n_dp):
        b = (dp - d + n_dp) % n_dp
        copy(qg_all.at[b], qg_all.at[b], e_ss.at[d - 1], e_rs.at[d - 1], dp_dev(b)).wait_recv()
        copy(fac_all.at[b], fac_all.at[b], f_ss.at[d - 1], f_rs.at[d - 1], dp_dev(b)).wait_recv()
    qg_out[...] = qg_all[...]
    fac_out[...] = fac_all[...]

    for d in range(1, n_ctx):
        j = (me - d + n_ctx) % n_ctx
        copy(gq_recv.at[j], gq_recv.at[j], o_ss.at[d - 1], o_rs.at[d - 1], ctx_dev(j)).wait_recv()
    gq_out[...] = gq_recv[...]

    total = inner_sum(nz - 1)
    for k in range(nz - 1):
        copy(z_recv.at[k], z_recv.at[k], kz_ss.at[k], kz_rs.at[k], ctx_dev(me)).wait_recv()
        total = total + z_recv[k].astype(F32)
    gl_out[...] = total
    for s in sends:
        s.wait_send()


def finish(fac_ref, qg_ref, gq_ref, gl_ref, gq_out, gl_out, gw_out):
    n_dp, hb, nq, wide = qg_ref.shape
    cr = gw_out.shape[0]

    @pl.when(pl.program_id(0) == 0)
    def _():
        gl_out[0] = gl_ref[...]
        n_ctx, _, wq = gq_ref.shape
        for j in range(n_ctx):
            gq_out[0, :, j * wq : (j + 1) * wq] = gq_ref[j]

    for h in range(hb):
        left = fac_ref[:, h * nq : (h + 1) * nq, :].reshape(n_dp * nq, 2 * cr)
        right = qg_ref[:, h].reshape(n_dp * nq, wide)
        both = dot(left, right, 0, 0)
        at = h * wide
        gw_out[:, at : at + DN] = both[:cr, :DN]
        gw_out[:, at + DN : at + wide] = both[cr:, DN:]


def local(n_dp, n_ctx, queries, grad_out, latent, latent_up, query_start, key_lengths):
    nz, ny = grid_of(n_ctx)
    rq = queries.shape[1]
    nq = rq * n_ctx
    wq = queries.shape[2] // n_ctx
    wv = grad_out.shape[2] // n_ctx
    heads = wv // DV
    rows = heads * nq
    lb = latent.shape[1]
    nk = lb * n_ctx
    cr = C // n_dp
    full = C + DR
    wide = DN + DV
    vm = pltpu.VMEM
    dma = pltpu.SemaphoreType.DMA
    spec = pl.BlockSpec(memory_space=pltpu.VMEM)
    smem = pl.BlockSpec(memory_space=pltpu.SMEM)
    n1 = n_ctx - 1
    d1 = max(n_dp - 1, 1)
    ys = max((ny - 1) * nz, 1)
    zs = max(nz - 1, 1)
    gq, gl, fac, qg = pl.pallas_call(
        functools.partial(kernel, n_dp, n_ctx),
        out_shape=(
            jax.ShapeDtypeStruct((n_ctx, rq, wq), F32),
            jax.ShapeDtypeStruct((full, lb), F32),
            jax.ShapeDtypeStruct((n_dp, rows, 2 * cr), BF16),
            jax.ShapeDtypeStruct((n_dp, heads, nq, wide), BF16),
        ),
        in_specs=[smem, smem, spec, spec, spec, pl.BlockSpec(memory_space=pltpu.HBM)],
        out_specs=(spec, spec, spec, spec),
        scratch_shapes=[
            vm(latent_up.shape, BF16),
            vm((n_ctx, rq, wq), BF16),
            vm((n_ctx, rq, wv), BF16),
            vm((nq, wq), F32),
            vm((nq, wv), F32),
            vm((n_dp, heads, nq, wide), BF16),
            vm((rows, full), BF16),
            vm((rows, C), BF16),
            vm((full, 2 * rows), BF16),
            vm((full, nk), BF16),
            vm((rows, nk), F32),
            vm((rows, nk), F32),
            vm((2 * rows, nk), BF16),
            vm((rows, C), BF16),
            vm((rows, DR), F32),
            vm((n_dp, rows, 2 * cr), BF16),
            vm((n_dp, rows, 2 * cr), BF16),
            vm((ys, full, lb), BF16),
            vm((ys, full, lb), BF16),
            vm((nz, full, lb), F32),
            vm((zs, full, lb), BF16),
            vm((zs, full, lb), BF16),
            vm((nq, wq), F32),
            vm((n_ctx, rq, wq), F32),
            vm((n_ctx, rq, wq), F32),
            dma,
            dma((n1,)), dma((n1,)), dma((n1,)), dma((n1,)),
            dma((zs,)), dma((zs,)), dma((ys,)), dma((ys,)),
            dma((d1,)), dma((d1,)), dma((d1,)), dma((d1,)),
            dma((ys,)), dma((ys,)), dma((zs,)), dma((zs,)),
            dma((n1,)), dma((n1,)),
        ],
        compiler_params=pltpu.CompilerParams(
            collective_id=0, has_side_effects=True, vmem_limit_bytes=40 * 1024 * 1024
        ),
    )(query_start, key_lengths, queries, grad_out, jnp.swapaxes(latent, 1, 2), latent_up)
    steps = 4 if heads % 4 == 0 else 1
    hb = heads // steps

    def same(k):
        return lambda i: (0,) * k

    grad_queries, grad_latent, grad_up = pl.pallas_call(
        finish,
        grid=(steps,),
        out_shape=(
            jax.ShapeDtypeStruct(queries.shape, F32),
            jax.ShapeDtypeStruct((1, full, lb), F32),
            jax.ShapeDtypeStruct((cr, latent_up.shape[1]), F32),
        ),
        in_specs=[
            pl.BlockSpec((n_dp, hb * nq, 2 * cr), lambda i: (0, i, 0)),
            pl.BlockSpec((n_dp, hb, nq, wide), lambda i: (0, i, 0, 0)),
            pl.BlockSpec((n_ctx, rq, wq), same(3)),
            pl.BlockSpec((full, lb), same(2)),
        ],
        out_specs=(
            pl.BlockSpec(queries.shape, same(3)),
            pl.BlockSpec((1, full, lb), same(3)),
            pl.BlockSpec((cr, hb * wide), lambda i: (0, i)),
        ),
        compiler_params=pltpu.CompilerParams(vmem_limit_bytes=16 * 1024 * 1024),
    )(fac, qg, gq, gl)
    return grad_queries, jnp.swapaxes(grad_latent, 1, 2), grad_up


def solution(mesh):
    return jax.shard_map(
        functools.partial(local, mesh.shape["dp"], mesh.shape["ctx"]),
        mesh=mesh,
        in_specs=(
            P("dp", "ctx", None),
            P("dp", "ctx", None),
            P("dp", "ctx", None),
            P(None, "ctx"),
            P("dp"),
            P("dp"),
        ),
        out_specs=(P("dp", "ctx", None), P("dp", "ctx", None), P("dp", "ctx")),
        check_vma=False,
    )
```

```python
import functools
import math

import jax
import jax.numpy as jnp
from jax import lax
from jax.experimental import pallas as pl
from jax.experimental.pallas import tpu as pltpu
from jax.sharding import PartitionSpec as P

DN = 128
DR = 64
DV = 128
C = 512

MSCALE = 0.1 * math.log(40.0) + 1.0
NEG_FILL = -1e30
SCALE = MSCALE * MSCALE / math.sqrt(DN + DR)
MESH = pl.DeviceIdType.MESH
F32 = jnp.float32
BF16 = jnp.bfloat16


def dot(a, b, da, db):
    return lax.dot_general(a, b, (((da,), (db,)), ((), ())), preferred_element_type=F32)


def grid_of(n):
    inner = 1
    while (2 * inner) ** 2 <= n and n % (2 * inner) == 0:
        inner *= 2
    return n // inner, inner


def kernel(
    n_dp, n_ctx, start_ref, length_ref, q_ref, g_ref, lat_ref, w_hbm,
    gq_out, gl_out, fac_out, qg_out,
    w, q_recv, g_recv, q_rows, g_rows, qg_all, q_full, g_lat, sides_t, keys,
    raw, grad_probs, low_all, grad_lat, rope_grad, fac_send, fac_all,
    kt_send, kt_recv, kt_own, z_send, z_recv, gq_rows, gq_send, gq_recv,
    w_sem, own_sem, q_ss, q_rs, g_ss, g_rs, az_ss, az_rs, ay_ss, ay_rs,
    e_ss, e_rs, f_ss, f_rs, ky_ss, ky_rs, kz_ss, kz_rs, o_ss, o_rs,
):
    nz, ny = grid_of(n_ctx)
    dp = lax.axis_index("dp")
    me = lax.axis_index("ctx")
    z, y = me // ny, me % ny
    rq = q_ref.shape[1]
    nq = rq * n_ctx
    wq = q_ref.shape[2] // n_ctx
    wv = g_ref.shape[2] // n_ctx
    heads = wv // DV
    rows = heads * nq
    lb = lat_ref.shape[2]
    nk = lb * n_ctx
    cr = C // n_dp

    def ctx_dev(i):
        return (dp, i)

    def dp_dev(i):
        return (i, me)

    def copy(src, dst, ss, rs, dev):
        return pltpu.make_async_remote_copy(
            src_ref=src, dst_ref=dst, send_sem=ss, recv_sem=rs, device_id=dev, device_id_type=MESH
        )

    def cols(block):
        return pl.ds(pl.multiple_of(block * lb, lb), lb)

    w_copy = pltpu.make_async_copy(w_hbm, w, w_sem)
    mine = pl.ds(pl.multiple_of(me * wq, 128), wq)
    own_q = pltpu.make_async_copy(q_ref.at[0, :, mine], q_recv.at[me], own_sem.at[0])
    mine = pl.ds(pl.multiple_of(me * wv, 128), wv)
    own_g = pltpu.make_async_copy(g_ref.at[0, :, mine], g_recv.at[me], own_sem.at[1])
    own_k = pltpu.make_async_copy(lat_ref.at[0], keys.at[:, cols(me)], own_sem.at[2])
    for own in (own_q, own_g, own_k, w_copy):
        own.start()

    barrier = pltpu.get_barrier_semaphore()
    peers = [ctx_dev((me + d) % n_ctx) for d in range(1, n_ctx)]
    peers += [dp_dev((dp + d) % n_dp) for d in range(1, n_dp)]
    for dev in peers:
        pl.semaphore_signal(barrier, inc=1, device_id=dev, device_id_type=MESH)
    pl.semaphore_wait(barrier, len(peers))

    sends = []

    def send(*args):
        copy(*args).start()
        sends.append((None, args))

    def send_if(cond, *args):
        @pl.when(cond)
        def _():
            copy(*args).start()

        sends.append((cond, args))

    for d in range(1, n_ctx):
        j = (me + d) % n_ctx
        at = pl.ds(pl.multiple_of(j * wq, 128), wq)
        send(q_ref.at[0, :, at], q_recv.at[me], q_ss.at[d - 1], q_rs.at[d - 1], ctx_dev(j))
        at = pl.ds(pl.multiple_of(j * wv, 128), wv)
        send(g_ref.at[0, :, at], g_recv.at[me], g_ss.at[d - 1], g_rs.at[d - 1], ctx_dev(j))

    hops = nz - 1
    steps = (1, -1)

    def inner(k, cond, src, block):
        for d in range(1, ny):
            to = z * ny + (y + d) % ny
            i = (d - 1) * (2 * hops + 1) + k
            args = (src, keys.at[:, cols(block)], ay_ss.at[i], ay_rs.at[i], ctx_dev(to))
            if cond is None:
                send(*args)
            else:
                send_if(cond, *args)

    def outer(line, t, has, src, block):
        to = z + steps[line]
        ok = has & (to >= 0) & (to < nz)
        i = line * hops + t
        send_if(ok, src, keys.at[:, cols(block)], az_ss.at[i], az_rs.at[i], ctx_dev(jnp.clip(to, 0, nz - 1) * ny + y))

    def from_outer(line, t):
        at = z - steps[line] * t
        return (at >= 0) & (at < nz), jnp.clip(at, 0, nz - 1) * ny

    if hops:
        for line in range(2):
            outer(line, 0, z >= 0, lat_ref.at[0], me)
    inner(0, None, lat_ref.at[0], me)

    def outer_in(t):
        for line in range(2):
            has, base = from_outer(line, t)
            block = base + y
            ref = keys.at[:, cols(block)]
            i = line * hops + t - 1

            @pl.when(has)
            def _(ref=ref, i=i):
                copy(ref, ref, az_ss.at[i], az_rs.at[i], ctx_dev(me)).wait_recv()

            if t < hops:
                outer(line, t, has, ref, block)
            inner(1 + i, has, ref, block)

    own_q.wait()
    own_g.wait()
    own_k.wait()
    for d in range(1, n_ctx):
        j = (me - d + n_ctx) % n_ctx
        copy(q_recv.at[j], q_recv.at[j], q_ss.at[d - 1], q_rs.at[d - 1], ctx_dev(j)).wait_recv()
        copy(g_recv.at[j], g_recv.at[j], g_ss.at[d - 1], g_rs.at[d - 1], ctx_dev(j)).wait_recv()
    for j in range(n_ctx):
        q_rows[rq * j : rq * (j + 1), :] = q_recv[j].astype(F32)
        g_rows[rq * j : rq * (j + 1), :] = g_recv[j].astype(F32)
    w_copy.wait()

    def latents(h):
        at = slice(h * nq, (h + 1) * nq)
        qh = q_rows[:, h * (DN + DR) : (h + 1) * (DN + DR)].astype(BF16)
        gh = g_rows[:, h * DV : (h + 1) * DV].astype(BF16)
        qg_all[dp, h, :, :DN] = qh[:, :DN]
        qg_all[dp, h, :, DN:] = gh
        col = h * (DN + DV)
        q_full[at, :C] = dot(qh[:, :DN], w[:, col : col + DN], 1, 1).astype(BF16)
        q_full[at, C:] = qh[:, DN:]
        g_lat[at, :] = dot(gh, w[:, col + DN : col + DN + DV], 1, 1).astype(BF16)

    done = 1
    per = -(-heads // nz)
    for h in range(heads):
        latents(h)
        if (h + 1) % per == 0 and done < nz:
            outer_in(done)
            done += 1
    for d in range(1, n_dp):
        send(qg_all.at[dp], qg_all.at[dp], e_ss.at[d - 1], e_rs.at[d - 1], dp_dev((dp + d) % n_dp))
    for d in range(done, nz):
        outer_in(d)

    def score_block(block):
        at = cols(block)
        part = keys[:, at]
        raw[:, at] = dot(q_full[...], part, 1, 0)
        grad_probs[:, at] = dot(g_lat[...], part[:C], 1, 0)

    for k in range(nz):
        score_block(((z - k + nz) % nz) * ny + y)
    sides_t[:C, :rows] = q_full[:, :C].T
    sides_t[C:, :rows] = q_full[:, C:].T
    sides_t[:C, rows:] = g_lat[...].T
    sides_t[C:, rows:] = jnp.zeros((DR, rows), BF16)
    for d in range(1, ny):
        yi = (y - d + ny) % ny
        base = (d - 1) * (2 * hops + 1)
        ref = keys.at[:, cols(z * ny + yi)]
        copy(ref, ref, ay_ss.at[base], ay_rs.at[base], ctx_dev(me)).wait_recv()
        score_block(z * ny + yi)
    for t in range(1, nz):
        for line in range(2):
            has, first = from_outer(line, t)
            for d in range(1, ny):
                block = first + (y - d + ny) % ny
                i = (d - 1) * (2 * hops + 1) + 1 + line * hops + t - 1

                @pl.when(has)
                def _(block=block, i=i):
                    ref = keys.at[:, cols(block)]
                    copy(ref, ref, ay_ss.at[i], ay_rs.at[i], ctx_dev(me)).wait_recv()
                    score_block(block)

    start = start_ref[0]
    low = start + nq - length_ref[0]
    rc = max(nq, 32)
    for c in range(rows // rc):
        at = slice(c * rc, (c + 1) * rc)
        key_pos = lax.broadcasted_iota(jnp.int32, (rc, nk), 1)
        row_pos = start + lax.broadcasted_iota(jnp.int32, (rc, nk), 0) % nq
        visible = (key_pos >= low) & (key_pos <= row_pos)
        masked = jnp.where(visible, raw[at, :] * SCALE, NEG_FILL)
        peak = jnp.max(masked, axis=1, keepdims=True)
        weights = jnp.where(visible, jnp.exp(masked - peak), 0.0)
        attn = weights * (1.0 / jnp.sum(weights, axis=1, keepdims=True))
        probs_low = attn.astype(BF16)
        gp = grad_probs[at, :]
        row_dot = jnp.sum(probs_low.astype(F32) * gp, axis=1, keepdims=True)
        low_all[at, :] = (SCALE * attn * (gp - row_dot)).astype(BF16)
        low_all[rows + c * rc : rows + (c + 1) * rc, :] = probs_low

    def key_block(block):
        return dot(sides_t[...], low_all[:, cols(block)], 1, 0)

    for k in range(nz):
        for d in range(1, ny):
            yi = (y + d) % ny
            i = (d - 1) * nz + k
            kt_send[i] = key_block(((z + k + 1) % nz) * ny + yi).astype(BF16)
            send(kt_send.at[i], kt_recv.at[i], ky_ss.at[i], ky_rs.at[i], ctx_dev(z * ny + yi))

    query_grad = dot(low_all[:rows, :], keys[...], 1, 1)
    rope_grad[...] = query_grad[:, C:]
    grad_lat[...] = query_grad[:, :C].astype(BF16)
    o_low = dot(low_all[rows:, :], keys[:C, :], 1, 1).astype(BF16)
    for b in range(n_dp):
        fac_send[b, :, :cr] = grad_lat[:, b * cr : (b + 1) * cr]
        fac_send[b, :, cr:] = o_low[:, b * cr : (b + 1) * cr]
    for d in range(1, n_dp):
        b = (dp + d) % n_dp
        send(fac_send.at[b], fac_all.at[dp], f_ss.at[d - 1], f_rs.at[d - 1], dp_dev(b))
    fac_all[dp] = fac_send[dp]

    def inner_sum(k):
        total = kt_own[k]
        for d in range(1, ny):
            i = (d - 1) * nz + k
            copy(kt_recv.at[i], kt_recv.at[i], ky_ss.at[i], ky_rs.at[i], ctx_dev(me)).wait_recv()
            total = total + kt_recv[i].astype(F32)
        return total

    for k in range(nz):
        kt_own[k] = key_block(((z + k + 1) % nz) * ny + y)
    for k in range(nz - 1):
        z_send[k] = inner_sum(k).astype(BF16)
        to = ((z + k + 1) % nz) * ny + y
        send(z_send.at[k], z_recv.at[k], kz_ss.at[k], kz_rs.at[k], ctx_dev(to))

    for h in range(heads):
        at = slice(h * nq, (h + 1) * nq)
        col = h * (DN + DV)
        to = h * (DN + DR)
        gq_rows[:, to : to + DN] = dot(grad_lat[at, :], w[:, col : col + DN], 1, 0)
        gq_rows[:, to + DN : to + DN + DR] = rope_grad[at, :]
    for j in range(n_ctx):
        gq_send[j] = gq_rows[rq * j : rq * (j + 1), :]
    for d in range(1, n_ctx):
        j = (me + d) % n_ctx
        send(gq_send.at[j], gq_recv.at[me], o_ss.at[d - 1], o_rs.at[d - 1], ctx_dev(j))
    gq_recv[me] = gq_send[me]

    for d in range(1, n_dp):
        b = (dp - d + n_dp) % n_dp
        copy(qg_all.at[b], qg_all.at[b], e_ss.at[d - 1], e_rs.at[d - 1], dp_dev(b)).wait_recv()
        copy(fac_all.at[b], fac_all.at[b], f_ss.at[d - 1], f_rs.at[d - 1], dp_dev(b)).wait_recv()
    qg_out[...] = qg_all[...]
    fac_out[...] = fac_all[...]

    for d in range(1, n_ctx):
        j = (me - d + n_ctx) % n_ctx
        copy(gq_recv.at[j], gq_recv.at[j], o_ss.at[d - 1], o_rs.at[d - 1], ctx_dev(j)).wait_recv()
    gq_out[...] = gq_recv[...]

    total = inner_sum(nz - 1)
    for k in range(nz - 1):
        copy(z_recv.at[k], z_recv.at[k], kz_ss.at[k], kz_rs.at[k], ctx_dev(me)).wait_recv()
        total = total + z_recv[k].astype(F32)
    gl_out[...] = total
    for cond, args in sends:
        if cond is None:
            copy(*args).wait_send()
        else:

            @pl.when(cond)
            def _(args=args):
                copy(*args).wait_send()


def finish(fac_ref, qg_ref, gq_ref, gl_ref, gq_out, gl_out, gw_out):
    n_dp, hb, nq, wide = qg_ref.shape
    cr = gw_out.shape[0]

    @pl.when(pl.program_id(0) == 0)
    def _():
        gl_out[0] = gl_ref[...]
        n_ctx, _, wq = gq_ref.shape
        for j in range(n_ctx):
            gq_out[0, :, j * wq : (j + 1) * wq] = gq_ref[j]

    for h in range(hb):
        left = fac_ref[:, h * nq : (h + 1) * nq, :].reshape(n_dp * nq, 2 * cr)
        right = qg_ref[:, h].reshape(n_dp * nq, wide)
        both = dot(left, right, 0, 0)
        at = h * wide
        gw_out[:, at : at + DN] = both[:cr, :DN]
        gw_out[:, at + DN : at + wide] = both[cr:, DN:]


def local(n_dp, n_ctx, queries, grad_out, latent, latent_up, query_start, key_lengths):
    nz, ny = grid_of(n_ctx)
    rq = queries.shape[1]
    nq = rq * n_ctx
    wq = queries.shape[2] // n_ctx
    wv = grad_out.shape[2] // n_ctx
    heads = wv // DV
    rows = heads * nq
    lb = latent.shape[1]
    nk = lb * n_ctx
    cr = C // n_dp
    full = C + DR
    wide = DN + DV
    vm = pltpu.VMEM
    dma = pltpu.SemaphoreType.DMA
    spec = pl.BlockSpec(memory_space=pltpu.VMEM)
    smem = pl.BlockSpec(memory_space=pltpu.SMEM)
    n1 = n_ctx - 1
    d1 = max(n_dp - 1, 1)
    ys = max((ny - 1) * nz, 1)
    zs = max(nz - 1, 1)
    as_ = max((ny - 1) * (2 * nz - 1), 1)
    gq, gl, fac, qg = pl.pallas_call(
        functools.partial(kernel, n_dp, n_ctx),
        out_shape=(
            jax.ShapeDtypeStruct((n_ctx, rq, wq), F32),
            jax.ShapeDtypeStruct((full, lb), F32),
            jax.ShapeDtypeStruct((n_dp, rows, 2 * cr), BF16),
            jax.ShapeDtypeStruct((n_dp, heads, nq, wide), BF16),
        ),
        in_specs=[smem, smem] + [pl.BlockSpec(memory_space=pltpu.HBM)] * 4,
        out_specs=(spec, spec, spec, spec),
        scratch_shapes=[
            vm(latent_up.shape, BF16),
            vm((n_ctx, rq, wq), BF16),
            vm((n_ctx, rq, wv), BF16),
            vm((nq, wq), F32),
            vm((nq, wv), F32),
            vm((n_dp, heads, nq, wide), BF16),
            vm((rows, full), BF16),
            vm((rows, C), BF16),
            vm((full, 2 * rows), BF16),
            vm((full, nk), BF16),
            vm((rows, nk), F32),
            vm((rows, nk), F32),
            vm((2 * rows, nk), BF16),
            vm((rows, C), BF16),
            vm((rows, DR), F32),
            vm((n_dp, rows, 2 * cr), BF16),
            vm((n_dp, rows, 2 * cr), BF16),
            vm((ys, full, lb), BF16),
            vm((ys, full, lb), BF16),
            vm((nz, full, lb), F32),
            vm((zs, full, lb), BF16),
            vm((zs, full, lb), BF16),
            vm((nq, wq), F32),
            vm((n_ctx, rq, wq), F32),
            vm((n_ctx, rq, wq), F32),
            dma, dma((3,)),
            dma((n1,)), dma((n1,)), dma((n1,)), dma((n1,)),
            dma((2 * zs,)), dma((2 * zs,)), dma((as_,)), dma((as_,)),
            dma((d1,)), dma((d1,)), dma((d1,)), dma((d1,)),
            dma((ys,)), dma((ys,)), dma((zs,)), dma((zs,)),
            dma((n1,)), dma((n1,)),
        ],
        compiler_params=pltpu.CompilerParams(
            collective_id=0, has_side_effects=True, vmem_limit_bytes=40 * 1024 * 1024
        ),
    )(query_start, key_lengths, *[pltpu.with_memory_space_constraint(v, pltpu.HBM) for v in (queries, grad_out, jnp.swapaxes(latent, 1, 2), latent_up)])
    steps = 4 if heads % 4 == 0 else 1
    hb = heads // steps

    def same(k):
        return lambda i: (0,) * k

    grad_queries, grad_latent, grad_up = pl.pallas_call(
        finish,
        grid=(steps,),
        out_shape=(
            jax.ShapeDtypeStruct(queries.shape, F32),
            jax.ShapeDtypeStruct((1, full, lb), F32),
            jax.ShapeDtypeStruct((cr, latent_up.shape[1]), F32),
        ),
        in_specs=[
            pl.BlockSpec((n_dp, hb * nq, 2 * cr), lambda i: (0, i, 0)),
            pl.BlockSpec((n_dp, hb, nq, wide), lambda i: (0, i, 0, 0)),
            pl.BlockSpec((n_ctx, rq, wq), same(3)),
            pl.BlockSpec((full, lb), same(2)),
        ],
        out_specs=(
            pl.BlockSpec(queries.shape, same(3)),
            pl.BlockSpec((1, full, lb), same(3)),
            pl.BlockSpec((cr, hb * wide), lambda i: (0, i)),
        ),
        compiler_params=pltpu.CompilerParams(vmem_limit_bytes=16 * 1024 * 1024),
    )(fac, qg, gq, gl)
    return grad_queries, jnp.swapaxes(grad_latent, 1, 2), grad_up


def solution(mesh):
    return jax.shard_map(
        functools.partial(local, mesh.shape["dp"], mesh.shape["ctx"]),
        mesh=mesh,
        in_specs=(
            P("dp", "ctx", None),
            P("dp", "ctx", None),
            P("dp", "ctx", None),
            P(None, "ctx"),
            P("dp"),
            P("dp"),
        ),
        out_specs=(P("dp", "ctx", None), P("dp", "ctx", None), P("dp", "ctx")),
        check_vma=False,
    )
```

```python
import functools
import math

import jax
import jax.numpy as jnp
from jax import lax
from jax.experimental import pallas as pl
from jax.experimental.pallas import tpu as pltpu
from jax.sharding import PartitionSpec as P

DN = 128
DR = 64
DV = 128
C = 512

MSCALE = 0.1 * math.log(40.0) + 1.0
NEG_FILL = -1e30
SCALE = MSCALE * MSCALE / math.sqrt(DN + DR)
MESH = pl.DeviceIdType.MESH
F32 = jnp.float32
BF16 = jnp.bfloat16


def dot(a, b, da, db):
    return lax.dot_general(a, b, (((da,), (db,)), ((), ())), preferred_element_type=F32)


def grid_of(n):
    inner = 1
    while (2 * inner) ** 2 <= n and n % (2 * inner) == 0:
        inner *= 2
    return n // inner, inner


def kernel(
    n_dp, n_ctx, start_ref, length_ref, q_ref, g_ref, lat_ref, w_hbm,
    gq_out, gl_out, fac_out, qg_out,
    w, q_recv, g_recv, q_rows, g_rows, qg_all, q_full, g_lat, sides_t, keys,
    raw, grad_probs, low_all, grad_lat, rope_grad, fac_send, fac_all,
    kt_send, kt_recv, kt_own, z_send, z_recv, gq_rows, gq_send, gq_recv,
    w_sem, own_sem, q_ss, q_rs, g_ss, g_rs, az_ss, az_rs, ay_ss, ay_rs,
    e_ss, e_rs, f_ss, f_rs, ky_ss, ky_rs, kz_ss, kz_rs, o_ss, o_rs,
):
    nz, ny = grid_of(n_ctx)
    dp = lax.axis_index("dp")
    me = lax.axis_index("ctx")
    z, y = me // ny, me % ny
    rq = q_ref.shape[1]
    nq = rq * n_ctx
    wq = q_ref.shape[2] // n_ctx
    wv = g_ref.shape[2] // n_ctx
    heads = wv // DV
    rows = heads * nq
    lb = lat_ref.shape[2]
    nk = lb * n_ctx
    cr = C // n_dp

    def ctx_dev(i):
        return (dp, i)

    def dp_dev(i):
        return (i, me)

    def copy(src, dst, ss, rs, dev):
        return pltpu.make_async_remote_copy(
            src_ref=src, dst_ref=dst, send_sem=ss, recv_sem=rs, device_id=dev, device_id_type=MESH
        )

    def cols(block):
        return pl.ds(pl.multiple_of(block * lb, lb), lb)

    w_copy = pltpu.make_async_copy(w_hbm, w, w_sem)
    mine = pl.ds(pl.multiple_of(me * wq, 128), wq)
    own_q = pltpu.make_async_copy(q_ref.at[0, :, mine], q_recv.at[me], own_sem.at[0])
    mine = pl.ds(pl.multiple_of(me * wv, 128), wv)
    own_g = pltpu.make_async_copy(g_ref.at[0, :, mine], g_recv.at[me], own_sem.at[1])
    own_k = pltpu.make_async_copy(lat_ref.at[0], keys.at[:, cols(me)], own_sem.at[2])
    for own in (own_q, own_g, own_k, w_copy):
        own.start()

    barrier = pltpu.get_barrier_semaphore()
    peers = [ctx_dev((me + d) % n_ctx) for d in range(1, n_ctx)]
    peers += [dp_dev((dp + d) % n_dp) for d in range(1, n_dp)]
    for dev in peers:
        pl.semaphore_signal(barrier, inc=1, device_id=dev, device_id_type=MESH)
    pl.semaphore_wait(barrier, len(peers))

    sends = []

    def send(*args):
        copy(*args).start()
        sends.append((None, args))

    def send_if(cond, *args):
        @pl.when(cond)
        def _():
            copy(*args).start()

        sends.append((cond, args))

    for d in range(1, n_ctx):
        j = (me + d) % n_ctx
        at = pl.ds(pl.multiple_of(j * wq, 128), wq)
        send(q_ref.at[0, :, at], q_recv.at[me], q_ss.at[d - 1], q_rs.at[d - 1], ctx_dev(j))
        at = pl.ds(pl.multiple_of(j * wv, 128), wv)
        send(g_ref.at[0, :, at], g_recv.at[me], g_ss.at[d - 1], g_rs.at[d - 1], ctx_dev(j))

    hops = nz - 1
    steps = (1, -1)

    def inner(k, cond, src, block):
        for d in range(1, ny):
            to = z * ny + (y + d) % ny
            i = (d - 1) * (2 * hops + 1) + k
            args = (src, keys.at[:, cols(block)], ay_ss.at[i], ay_rs.at[i], ctx_dev(to))
            if cond is None:
                send(*args)
            else:
                send_if(cond, *args)

    def outer(line, t, has, src, block):
        to = z + steps[line]
        ok = has & (to >= 0) & (to < nz)
        i = line * hops + t
        send_if(ok, src, keys.at[:, cols(block)], az_ss.at[i], az_rs.at[i], ctx_dev(jnp.clip(to, 0, nz - 1) * ny + y))

    def from_outer(line, t):
        at = z - steps[line] * t
        return (at >= 0) & (at < nz), jnp.clip(at, 0, nz - 1) * ny

    if hops:
        for line in range(2):
            outer(line, 0, z >= 0, lat_ref.at[0], me)
    inner(0, None, lat_ref.at[0], me)

    def outer_in(t):
        for line in range(2):
            has, base = from_outer(line, t)
            block = base + y
            ref = keys.at[:, cols(block)]
            i = line * hops + t - 1

            @pl.when(has)
            def _(ref=ref, i=i):
                copy(ref, ref, az_ss.at[i], az_rs.at[i], ctx_dev(me)).wait_recv()

            if t < hops:
                outer(line, t, has, ref, block)
            inner(1 + i, has, ref, block)

    own_q.wait()
    own_g.wait()
    own_k.wait()
    for d in range(1, n_ctx):
        j = (me - d + n_ctx) % n_ctx
        copy(q_recv.at[j], q_recv.at[j], q_ss.at[d - 1], q_rs.at[d - 1], ctx_dev(j)).wait_recv()
        copy(g_recv.at[j], g_recv.at[j], g_ss.at[d - 1], g_rs.at[d - 1], ctx_dev(j)).wait_recv()
    for j in range(n_ctx):
        q_rows[rq * j : rq * (j + 1), :] = q_recv[j].astype(F32)
        g_rows[rq * j : rq * (j + 1), :] = g_recv[j].astype(F32)
    w_copy.wait()

    def latents(h):
        at = slice(h * nq, (h + 1) * nq)
        qh = q_rows[:, h * (DN + DR) : (h + 1) * (DN + DR)].astype(BF16)
        gh = g_rows[:, h * DV : (h + 1) * DV].astype(BF16)
        qg_all[dp, h, :, :DN] = qh[:, :DN]
        qg_all[dp, h, :, DN:] = gh
        col = h * (DN + DV)
        q_full[at, :C] = dot(qh[:, :DN], w[:, col : col + DN], 1, 1).astype(BF16)
        q_full[at, C:] = qh[:, DN:]
        g_lat[at, :] = dot(gh, w[:, col + DN : col + DN + DV], 1, 1).astype(BF16)

    done = 1
    per = -(-heads // nz)
    for h in range(heads):
        latents(h)
        if (h + 1) % per == 0 and done < nz:
            outer_in(done)
            done += 1
    for d in range(1, n_dp):
        send(qg_all.at[dp], qg_all.at[dp], e_ss.at[d - 1], e_rs.at[d - 1], dp_dev((dp + d) % n_dp))
    for d in range(done, nz):
        outer_in(d)

    def score_block(block):
        at = cols(block)
        part = keys[:, at]
        raw[:, at] = dot(q_full[...], part, 1, 0)
        grad_probs[:, at] = dot(g_lat[...], part[:C], 1, 0)

    for k in range(nz):
        score_block(((z - k + nz) % nz) * ny + y)
    sides_t[:C, :rows] = q_full[:, :C].T
    sides_t[C:, :rows] = q_full[:, C:].T
    sides_t[:C, rows:] = g_lat[...].T
    sides_t[C:, rows:] = jnp.zeros((DR, rows), BF16)
    for d in range(1, ny):
        yi = (y - d + ny) % ny
        base = (d - 1) * (2 * hops + 1)
        ref = keys.at[:, cols(z * ny + yi)]
        copy(ref, ref, ay_ss.at[base], ay_rs.at[base], ctx_dev(me)).wait_recv()
        score_block(z * ny + yi)
    for t in range(1, nz):
        for line in range(2):
            has, first = from_outer(line, t)
            for d in range(1, ny):
                block = first + (y - d + ny) % ny
                i = (d - 1) * (2 * hops + 1) + 1 + line * hops + t - 1

                @pl.when(has)
                def _(block=block, i=i):
                    ref = keys.at[:, cols(block)]
                    copy(ref, ref, ay_ss.at[i], ay_rs.at[i], ctx_dev(me)).wait_recv()
                    score_block(block)

    start = start_ref[0]
    low = start + nq - length_ref[0]
    rc = max(nq, 32)
    for c in range(rows // rc):
        at = slice(c * rc, (c + 1) * rc)
        key_pos = lax.broadcasted_iota(jnp.int32, (rc, nk), 1)
        row_pos = start + lax.broadcasted_iota(jnp.int32, (rc, nk), 0) % nq
        visible = (key_pos >= low) & (key_pos <= row_pos)
        masked = jnp.where(visible, raw[at, :] * SCALE, NEG_FILL)
        peak = jnp.max(masked, axis=1, keepdims=True)
        weights = jnp.where(visible, jnp.exp(masked - peak), 0.0)
        attn = weights * (1.0 / jnp.sum(weights, axis=1, keepdims=True))
        probs_low = attn.astype(BF16)
        gp = grad_probs[at, :]
        row_dot = jnp.sum(probs_low.astype(F32) * gp, axis=1, keepdims=True)
        low_all[at, :] = (SCALE * attn * (gp - row_dot)).astype(BF16)
        low_all[rows + c * rc : rows + (c + 1) * rc, :] = probs_low

    def key_block(block):
        return dot(sides_t[...], low_all[:, cols(block)], 1, 0)

    for k in range(nz):
        slot = jnp.where((2 * z < nz) & (k < nz - 1), nz - 2 - k, k)
        for d in range(1, ny):
            yi = (y + d) % ny
            i = (d - 1) * nz + slot
            kt_send[i] = key_block(((z + slot + 1) % nz) * ny + yi).astype(BF16)
            send(kt_send.at[i], kt_recv.at[i], ky_ss.at[i], ky_rs.at[i], ctx_dev(z * ny + yi))

    query_grad = dot(low_all[:rows, :], keys[...], 1, 1)
    rope_grad[...] = query_grad[:, C:]
    grad_lat[...] = query_grad[:, :C].astype(BF16)
    o_low = dot(low_all[rows:, :], keys[:C, :], 1, 1).astype(BF16)
    for b in range(n_dp):
        fac_send[b, :, :cr] = grad_lat[:, b * cr : (b + 1) * cr]
        fac_send[b, :, cr:] = o_low[:, b * cr : (b + 1) * cr]
    for d in range(1, n_dp):
        b = (dp + d) % n_dp
        send(fac_send.at[b], fac_all.at[dp], f_ss.at[d - 1], f_rs.at[d - 1], dp_dev(b))
    fac_all[dp] = fac_send[dp]

    def inner_sum(k):
        total = kt_own[k]
        for d in range(1, ny):
            i = (d - 1) * nz + k
            copy(kt_recv.at[i], kt_recv.at[i], ky_ss.at[i], ky_rs.at[i], ctx_dev(me)).wait_recv()
            total = total + kt_recv[i].astype(F32)
        return total

    for k in range(nz):
        kt_own[k] = key_block(((z + k + 1) % nz) * ny + y)
    for t in range(hops, 0, -1):
        for line in range(2):
            owner = z + steps[line] * t
            prev = z - steps[line]
            ok = (owner >= 0) & (owner < nz)
            i = line * hops + t - 1

            @pl.when(ok)
            def _(k=t - 1 if line == 0 else hops - t, i=i):
                kt_own[k] = inner_sum(k)

            if t < hops:

                @pl.when(ok & (prev >= 0) & (prev < nz))
                def _(k=t - 1 if line == 0 else hops - t, i=i):
                    copy(z_recv.at[i + 1], z_recv.at[i + 1], kz_ss.at[i + 1], kz_rs.at[i + 1], ctx_dev(me)).wait_recv()
                    kt_own[k] = kt_own[k] + z_recv[i + 1].astype(F32)

            @pl.when(ok)
            def _(k=t - 1 if line == 0 else hops - t, i=i):
                z_send[i] = kt_own[k].astype(BF16)

            to = jnp.clip(z + steps[line], 0, nz - 1) * ny + y
            send_if(ok, z_send.at[i], z_recv.at[i], kz_ss.at[i], kz_rs.at[i], ctx_dev(to))

    for h in range(heads):
        at = slice(h * nq, (h + 1) * nq)
        col = h * (DN + DV)
        to = h * (DN + DR)
        gq_rows[:, to : to + DN] = dot(grad_lat[at, :], w[:, col : col + DN], 1, 0)
        gq_rows[:, to + DN : to + DN + DR] = rope_grad[at, :]
    for j in range(n_ctx):
        gq_send[j] = gq_rows[rq * j : rq * (j + 1), :]
    for d in range(1, n_ctx):
        j = (me + d) % n_ctx
        send(gq_send.at[j], gq_recv.at[me], o_ss.at[d - 1], o_rs.at[d - 1], ctx_dev(j))
    gq_recv[me] = gq_send[me]

    for d in range(1, n_dp):
        b = (dp - d + n_dp) % n_dp
        copy(qg_all.at[b], qg_all.at[b], e_ss.at[d - 1], e_rs.at[d - 1], dp_dev(b)).wait_recv()
        copy(fac_all.at[b], fac_all.at[b], f_ss.at[d - 1], f_rs.at[d - 1], dp_dev(b)).wait_recv()
    qg_out[...] = qg_all[...]
    fac_out[...] = fac_all[...]

    for d in range(1, n_ctx):
        j = (me - d + n_ctx) % n_ctx
        copy(gq_recv.at[j], gq_recv.at[j], o_ss.at[d - 1], o_rs.at[d - 1], ctx_dev(j)).wait_recv()
    gq_out[...] = gq_recv[...]

    gl_out[...] = inner_sum(nz - 1)
    if hops:
        for line in range(2):
            prev = z - steps[line]

            @pl.when((prev >= 0) & (prev < nz))
            def _(i=line * hops):
                copy(z_recv.at[i], z_recv.at[i], kz_ss.at[i], kz_rs.at[i], ctx_dev(me)).wait_recv()
                gl_out[...] = gl_out[...] + z_recv[i].astype(F32)

    for cond, args in sends:
        if cond is None:
            copy(*args).wait_send()
        else:

            @pl.when(cond)
            def _(args=args):
                copy(*args).wait_send()


def finish(fac_ref, qg_ref, gq_ref, gl_ref, gq_out, gl_out, gw_out):
    n_dp, hb, nq, wide = qg_ref.shape
    cr = gw_out.shape[0]

    @pl.when(pl.program_id(0) == 0)
    def _():
        gl_out[0] = gl_ref[...]
        n_ctx, _, wq = gq_ref.shape
        for j in range(n_ctx):
            gq_out[0, :, j * wq : (j + 1) * wq] = gq_ref[j]

    for h in range(hb):
        left = fac_ref[:, h * nq : (h + 1) * nq, :].reshape(n_dp * nq, 2 * cr)
        right = qg_ref[:, h].reshape(n_dp * nq, wide)
        both = dot(left, right, 0, 0)
        at = h * wide
        gw_out[:, at : at + DN] = both[:cr, :DN]
        gw_out[:, at + DN : at + wide] = both[cr:, DN:]


def local(n_dp, n_ctx, queries, grad_out, latent, latent_up, query_start, key_lengths):
    nz, ny = grid_of(n_ctx)
    rq = queries.shape[1]
    nq = rq * n_ctx
    wq = queries.shape[2] // n_ctx
    wv = grad_out.shape[2] // n_ctx
    heads = wv // DV
    rows = heads * nq
    lb = latent.shape[1]
    nk = lb * n_ctx
    cr = C // n_dp
    full = C + DR
    wide = DN + DV
    vm = pltpu.VMEM
    dma = pltpu.SemaphoreType.DMA
    spec = pl.BlockSpec(memory_space=pltpu.VMEM)
    smem = pl.BlockSpec(memory_space=pltpu.SMEM)
    n1 = n_ctx - 1
    d1 = max(n_dp - 1, 1)
    ys = max((ny - 1) * nz, 1)
    zs = max(nz - 1, 1)
    as_ = max((ny - 1) * (2 * nz - 1), 1)
    gq, gl, fac, qg = pl.pallas_call(
        functools.partial(kernel, n_dp, n_ctx),
        out_shape=(
            jax.ShapeDtypeStruct((n_ctx, rq, wq), F32),
            jax.ShapeDtypeStruct((full, lb), F32),
            jax.ShapeDtypeStruct((n_dp, rows, 2 * cr), BF16),
            jax.ShapeDtypeStruct((n_dp, heads, nq, wide), BF16),
        ),
        in_specs=[smem, smem] + [pl.BlockSpec(memory_space=pltpu.HBM)] * 4,
        out_specs=(spec, spec, spec, spec),
        scratch_shapes=[
            vm(latent_up.shape, BF16),
            vm((n_ctx, rq, wq), BF16),
            vm((n_ctx, rq, wv), BF16),
            vm((nq, wq), F32),
            vm((nq, wv), F32),
            vm((n_dp, heads, nq, wide), BF16),
            vm((rows, full), BF16),
            vm((rows, C), BF16),
            vm((full, 2 * rows), BF16),
            vm((full, nk), BF16),
            vm((rows, nk), F32),
            vm((rows, nk), F32),
            vm((2 * rows, nk), BF16),
            vm((rows, C), BF16),
            vm((rows, DR), F32),
            vm((n_dp, rows, 2 * cr), BF16),
            vm((n_dp, rows, 2 * cr), BF16),
            vm((ys, full, lb), BF16),
            vm((ys, full, lb), BF16),
            vm((nz, full, lb), F32),
            vm((2 * zs, full, lb), BF16),
            vm((2 * zs, full, lb), BF16),
            vm((nq, wq), F32),
            vm((n_ctx, rq, wq), F32),
            vm((n_ctx, rq, wq), F32),
            dma, dma((3,)),
            dma((n1,)), dma((n1,)), dma((n1,)), dma((n1,)),
            dma((2 * zs,)), dma((2 * zs,)), dma((as_,)), dma((as_,)),
            dma((d1,)), dma((d1,)), dma((d1,)), dma((d1,)),
            dma((ys,)), dma((ys,)), dma((2 * zs,)), dma((2 * zs,)),
            dma((n1,)), dma((n1,)),
        ],
        compiler_params=pltpu.CompilerParams(
            collective_id=0, has_side_effects=True, vmem_limit_bytes=48 * 1024 * 1024
        ),
    )(query_start, key_lengths, *[pltpu.with_memory_space_constraint(v, pltpu.HBM) for v in (queries, grad_out, jnp.swapaxes(latent, 1, 2), latent_up)])
    steps = 4 if heads % 4 == 0 else 1
    hb = heads // steps

    def same(k):
        return lambda i: (0,) * k

    grad_queries, grad_latent, grad_up = pl.pallas_call(
        finish,
        grid=(steps,),
        out_shape=(
            jax.ShapeDtypeStruct(queries.shape, F32),
            jax.ShapeDtypeStruct((1, full, lb), F32),
            jax.ShapeDtypeStruct((cr, latent_up.shape[1]), F32),
        ),
        in_specs=[
            pl.BlockSpec((n_dp, hb * nq, 2 * cr), lambda i: (0, i, 0)),
            pl.BlockSpec((n_dp, hb, nq, wide), lambda i: (0, i, 0, 0)),
            pl.BlockSpec((n_ctx, rq, wq), same(3)),
            pl.BlockSpec((full, lb), same(2)),
        ],
        out_specs=(
            pl.BlockSpec(queries.shape, same(3)),
            pl.BlockSpec((1, full, lb), same(3)),
            pl.BlockSpec((cr, hb * wide), lambda i: (0, i)),
        ),
        compiler_params=pltpu.CompilerParams(vmem_limit_bytes=16 * 1024 * 1024),
    )(fac, qg, gq, gl)
    return grad_queries, jnp.swapaxes(grad_latent, 1, 2), grad_up


def solution(mesh):
    return jax.shard_map(
        functools.partial(local, mesh.shape["dp"], mesh.shape["ctx"]),
        mesh=mesh,
        in_specs=(
            P("dp", "ctx", None),
            P("dp", "ctx", None),
            P("dp", "ctx", None),
            P(None, "ctx"),
            P("dp"),
            P("dp"),
        ),
        out_specs=(P("dp", "ctx", None), P("dp", "ctx", None), P("dp", "ctx")),
        check_vma=False,
    )
```
